32 devices in a mesh: groups: 2 (over y), ctx: 16 (over z, x, core).
Axes of the slice: x: 2, y: 2, z: 4, core: 2. Of those that a mesh axis runs over, the one named last changes fastest.
Arguments:
- queries: bfloat16 [4096, 4096], P(('groups', 'ctx')), parts along dimension 0, may hold values from -6 to 6
- keys: bfloat16 [4096, 512], P(('groups', 'ctx')), parts along dimension 0, may hold values from -6 to 6
- values: bfloat16 [4096, 512], P(('groups', 'ctx')), parts along dimension 0, may hold values from -6 to 6
- out_grad: bfloat16 [4096, 4096], P(('groups', 'ctx')), parts along dimension 0, may hold values from -6 to 6
- attn_out: bfloat16 [4096, 4096], P(('groups', 'ctx')), parts along dimension 0, may hold values from -6 to 6
- doc_ids: int32 [4096], P(('groups', 'ctx')), parts along dimension 0, may hold values from 0 to 3, never falling along the last dimension, each value on 1 to 1024 neighbouring positions
Outputs:
- query_grad: bfloat16 [4096, 4096], P(('groups', 'ctx')), parts along dimension 0
- key_grad: bfloat16 [4096, 512], P(('groups', 'ctx')), parts along dimension 0
- value_gradient: bfloat16 [4096, 512], P(('groups', 'ctx')), parts along dimension 0
The draws below stay inside these ranges and needn't reach their ends.
There are 2 independent parts, one for each index of `groups`. The reference program is written for one: setup_inputs(seed, part) draws one part's arguments, and reference() takes and returns one part's arrays. A program takes and returns all parts, laid end to end along the dimension named above; each array names one. Nothing has to cross between parts.
Inputs may be any that keep to these rules, and one draw needn't show every extreme that they name: `doc_ids`: ids never fall along the sequence; every document has at most 1024 tokens and one has exactly 1024.
All inputs are finite; a program needn't handle non-finite values.
Results may differ from the reference program's by a relative error of at most 0.0055.
Values may be sent and summed in bfloat16 or wider, within the bound.
A program may use at most 128 MiB of HBM per device.

```python
import math
import jax
import jax.numpy as jnp
import numpy as np
from jax import lax

HEAD_DIM = 128
HEADS = 32
KV_HEADS = 4
TOKENS = 2048
MOST_DOC = 1024
DOCS = 4


def draw_queries(key, part):
    key = jax.random.fold_in(key, 11)
    field = jnp.clip(jax.random.normal(key, (TOKENS, HEADS, HEAD_DIM), jnp.float32), -4.0, 4.0)
    return field.reshape(TOKENS, HEADS * HEAD_DIM).astype(jnp.bfloat16)


def draw_keys(key, part):
    key = jax.random.fold_in(key, 12)
    field = jnp.clip(jax.random.normal(key, (TOKENS, KV_HEADS, HEAD_DIM), jnp.float32), -4.0, 4.0)
    return field.reshape(TOKENS, KV_HEADS * HEAD_DIM).astype(jnp.bfloat16)


def block_levels(own_key, dims, shards, smallest, high):
    level, own = 1.0, jax.random.fold_in(own_key, 6)
    for dim, blocks in shards:
        heights = jnp.exp(jax.random.uniform(jax.random.fold_in(own, dim), (blocks,), jnp.float32, smallest / len(shards), high / len(shards)))
        level = level * jnp.repeat(heights, dims[dim] // blocks).reshape([-1 if axis == dim else 1 for axis in range(len(dims))])
    return level


def profile(amount, total, reach, slope):
    portions = [(1 << 20) // math.isqrt(grade ** slope) + 1 for grade in range(2, amount + 1)]
    rest, holding = total - reach - (amount - 1), [1] * (amount - 1)
    while rest > 0:
        free = [i for i in range(amount - 1) if holding[i] < reach]
        whole, budget = sum([portions[i] for i in free]), rest
        for i in free:
            more = min(reach - holding[i], max(1, budget * portions[i] // whole), rest)
            holding[i] = holding[i] + more
            rest = rest - more
    return np.array([reach] + holding)


def ragged_sizes(stream_key, count, total, limit, slope):
    if count == 2:
        one = jax.random.randint(stream_key, (), max(1, total - limit), min(limit, total - 1) + 1)
        return jnp.stack([one, total - one])
    tallies = jnp.asarray(profile(count, total, limit, slope), jnp.int32)
    couples = (count - 1) // 2
    giver, sink = tallies[1:1 + 2 * couples:2], tallies[2:2 + 2 * couples:2]
    slack = jnp.minimum(giver - 1, limit - sink)
    moved = jax.random.randint(jax.random.fold_in(stream_key, 1), (couples,), 0, 1 << 20) % (slack + 1)
    tallies = tallies.at[1:1 + 2 * couples:2].set(giver - moved).at[2:2 + 2 * couples:2].set(sink + moved)
    return tallies[jax.random.permutation(jax.random.fold_in(stream_key, 2), count)]


def scatter_about(rng, dims, scale, limit, pieces=(), kind=jnp.bfloat16):
    result = jax.random.normal(rng, dims, jnp.float32) * scale
    if len(pieces) > 0:
        result = block_levels(rng, dims, pieces, -0.22, 0.18) * result
    return jnp.clip(result, min=-limit, max=limit).astype(kind)


def setup_inputs(seed: int = 0, part: int = 0) -> dict:
    key_list = jax.random.split(jax.random.key(seed), 7)
    own_keys = jax.random.split(jax.random.fold_in(key_list[6], part), 7)
    return {
        "queries": draw_queries(jax.random.fold_in(jax.random.fold_in(key_list[6], part), 71), part),
        "keys": draw_keys(jax.random.fold_in(jax.random.fold_in(key_list[6], part), 71), part),
        "values": scatter_about(own_keys[2], (TOKENS, KV_HEADS * HEAD_DIM), 1.0, 6.0, ((0, 16),)),
        "out_grad": scatter_about(own_keys[3], (TOKENS, HEADS * HEAD_DIM), 1.0, 6.0, ((0, 16),)),
        "attn_out": scatter_about(own_keys[4], (TOKENS, HEADS * HEAD_DIM), 1.0, 6.0, ((0, 16),)),
        "doc_ids": jnp.searchsorted(jnp.cumsum(ragged_sizes(own_keys[5], DOCS, TOKENS, MOST_DOC, 2)), jnp.arange(TOKENS), side="right").astype(jnp.int32),
    }


def reference(queries, keys, values, out_grad, attn_out, doc_ids):
    group_size = HEADS // KV_HEADS
    block_len = math.gcd(512, TOKENS)
    span_len = MOST_DOC + block_len
    block_count = TOKENS // block_len
    score_scale = 1.0 / math.sqrt(HEAD_DIM)
    query_heads = queries.reshape(TOKENS, HEADS, HEAD_DIM)
    grad_heads = out_grad.reshape(TOKENS, HEADS, HEAD_DIM)
    out_heads = attn_out.reshape(TOKENS, HEADS, HEAD_DIM)
    delta_all = lax.optimization_barrier(jnp.sum(grad_heads.astype(jnp.float32) * out_heads.astype(jnp.float32), axis=2))
    key_heads = keys.reshape(TOKENS, KV_HEADS, HEAD_DIM)
    value_heads = values.reshape(TOKENS, KV_HEADS, HEAD_DIM)
    lead_zeros = jnp.zeros((MOST_DOC, KV_HEADS, HEAD_DIM), keys.dtype)
    key_padded = jnp.concatenate([lead_zeros, key_heads], axis=0)
    value_padded = jnp.concatenate([lead_zeros, value_heads], axis=0)
    doc_shift = doc_ids + 1
    doc_padded = jnp.concatenate([jnp.zeros((MOST_DOC,), jnp.int32), doc_shift], axis=0)

    def one_block(totals, work_item):
        key_total, value_total = totals
        head_no = work_item // block_count
        start = work_item % block_count * block_len
        kv_no = head_no // group_size
        zero = jnp.zeros((), jnp.int32)
        query_rows = lax.dynamic_slice(query_heads, (start, head_no, zero), (block_len, 1, HEAD_DIM))[:, 0]
        grad_rows = lax.dynamic_slice(grad_heads, (start, head_no, zero), (block_len, 1, HEAD_DIM))[:, 0]
        delta_rows = lax.dynamic_slice(delta_all, (start, head_no), (block_len, 1))[:, 0]
        key_rows = lax.dynamic_slice(key_padded, (start, kv_no, zero), (span_len, 1, HEAD_DIM))[:, 0]
        value_rows = lax.dynamic_slice(value_padded, (start, kv_no, zero), (span_len, 1, HEAD_DIM))[:, 0]
        query_pos = start + jnp.arange(block_len, dtype=jnp.int32)
        key_pos = start - MOST_DOC + jnp.arange(span_len, dtype=jnp.int32)
        query_doc = lax.dynamic_slice(doc_shift, (start,), (block_len,))
        key_doc = lax.dynamic_slice(doc_padded, (start,), (span_len,))
        visible = (key_pos[None, :] <= query_pos[:, None]) & (key_doc[None, :] == query_doc[:, None])
        scores = jnp.dot(query_rows, key_rows.T, preferred_element_type=jnp.float32) * score_scale
        scores = jnp.where(visible, scores, -jnp.inf)
        row_max = lax.optimization_barrier(jnp.max(scores, axis=1, keepdims=True))
        raw_weights = jnp.where(visible, jnp.exp(scores - row_max), 0.0)
        softmax_w = raw_weights / lax.optimization_barrier(jnp.sum(raw_weights, axis=1, keepdims=True))
        probability_lowprec = softmax_w.astype(jnp.bfloat16)
        value_gradient = jnp.dot(probability_lowprec.T, grad_rows, preferred_element_type=jnp.float32)
        probability_gradient = jnp.dot(grad_rows, value_rows.T, preferred_element_type=jnp.float32)
        score_lowprec = (softmax_w * (probability_gradient - delta_rows[:, None])).astype(jnp.bfloat16)
        query_grad = (jnp.dot(score_lowprec, key_rows, preferred_element_type=jnp.float32) * score_scale).astype(jnp.bfloat16)
        key_grad = jnp.dot(score_lowprec.T, query_rows, preferred_element_type=jnp.float32) * score_scale
        key_now = lax.dynamic_slice(key_total, (start, kv_no, zero), (span_len, 1, HEAD_DIM))
        key_total = lax.dynamic_update_slice(key_total, key_now + key_grad[:, None, :], (start, kv_no, zero))
        value_now = lax.dynamic_slice(value_total, (start, kv_no, zero), (span_len, 1, HEAD_DIM))
        value_total = lax.dynamic_update_slice(value_total, value_now + value_gradient[:, None, :], (start, kv_no, zero))
        return ((key_total, value_total), query_grad)
    empty = jnp.zeros((TOKENS + MOST_DOC, KV_HEADS, HEAD_DIM), jnp.float32)
    totals, query_blocks = lax.scan(one_block, (empty, empty), jnp.arange(HEADS * block_count, dtype=jnp.int32))
    query_grad = query_blocks.reshape(HEADS, TOKENS, HEAD_DIM).transpose(1, 0, 2).reshape(TOKENS, HEADS * HEAD_DIM)
    key_grad = totals[0][MOST_DOC:].reshape(TOKENS, KV_HEADS * HEAD_DIM).astype(jnp.bfloat16)
    value_gradient = totals[1][MOST_DOC:].reshape(TOKENS, KV_HEADS * HEAD_DIM).astype(jnp.bfloat16)
    return (query_grad, key_grad, value_gradient)
```

```python
import functools
import math

import jax
import jax.numpy as jnp
from jax import lax
from jax.experimental import pallas as pl
from jax.experimental.pallas import tpu as pltpu
from jax.sharding import PartitionSpec as P

HEAD_DIM = 128
HEADS = 32
KV_HEADS = 4
BLOCKS = 9
EVENS = 5
PAIRS = 4
DOC_ROWS = 16


def to(rank):
    return dict(device_id={"ctx": rank}, device_id_type=pl.DeviceIdType.MESH)


def kernel(
    ranks,
    q_ref,
    k_ref,
    v_ref,
    g_ref,
    o_ref,
    doc_ref,
    dq_ref,
    dk_ref,
    dv_ref,
    win,
    bias,
    acc_k,
    acc_v,
    sum_k,
    sum_v,
    sib_out,
    sib_in,
    x_out,
    x_in,
    z_out,
    z_in,
    in_send,
    in_recv,
    back_send,
    back_recv,
):
    rows = q_ref.shape[0]
    span = BLOCKS * rows
    scale = 1.0 / math.sqrt(HEAD_DIM)
    exp_scale = scale * math.log2(math.e)
    rank = lax.axis_index("ctx")
    core = rank % 2
    col = (rank // 2) % 2
    sibling = rank + 1 - 2 * core
    partner = rank + 2 - 4 * col
    up4, up8 = rank + 4 < ranks, rank + 8 < ranks
    down4, down8 = rank >= 4, rank >= 8

    barrier = pltpu.get_barrier_semaphore()
    for peer in (sibling, partner):
        pl.semaphore_signal(barrier, inc=1, **to(peer))
    for there, peer in ((up4, rank + 4), (up8, rank + 8), (down4, rank - 4), (down8, rank - 8)):

        @pl.when(there)
        def _(peer=peer):
            pl.semaphore_signal(barrier, inc=1, **to(peer))

    own_doc = doc_ref[...].astype(jnp.float32)
    for g in range(KV_HEADS):
        cols = slice(g * HEAD_DIM, (g + 1) * HEAD_DIM)
        win[g, 0, 0:rows, :] = k_ref[:, cols]
        win[g, 0, rows : 2 * rows, :] = v_ref[:, cols]
        win[g, 0, 2 * rows :, :] = jnp.broadcast_to(own_doc, (DOC_ROWS, rows)).astype(jnp.bfloat16)
        for slot, there in ((2, down4), (4, down8)):

            @pl.when(jnp.logical_not(there))
            def _(g=g, slot=slot):
                win[g, slot, 0 : 2 * rows, :] = jnp.zeros((2 * rows, HEAD_DIM), jnp.bfloat16)
                win[g, slot, 2 * rows :, :] = jnp.full((DOC_ROWS, HEAD_DIM), -1.0, jnp.bfloat16)

    near = [there.astype(jnp.int32) for there in (up4, up8, down4, down8)]
    pl.semaphore_wait(barrier, 2 + sum(near))

    def in_z(g, step):
        return pltpu.make_async_remote_copy(
            src_ref=win.at[g, 0],
            dst_ref=win.at[g, 2 * step],
            send_sem=in_send.at[g, step - 1],
            recv_sem=in_recv.at[g, step - 1],
            **to(rank + 4 * step),
        )

    def in_x(g, half):
        return pltpu.make_async_remote_copy(
            src_ref=win.at[g, 2 * col + 2 * half],
            dst_ref=win.at[g, 1 + 2 * half],
            send_sem=in_send.at[g, 2 + half],
            recv_sem=in_recv.at[g, 2 + half],
            **to(partner),
        )

    def in_sib(g):
        return pltpu.make_async_remote_copy(
            src_ref=win.at[g, pl.ds(core, 4)],
            dst_ref=win.at[g, pl.ds(EVENS, 4)],
            send_sem=in_send.at[g, 4],
            recv_sem=in_recv.at[g, 4],
            **to(sibling),
        )

    def start_z(g):
        @pl.when(up4)
        def _():
            in_z(g, 1).start()

        @pl.when(up8)
        def _():
            in_z(g, 2).start()

    def start_x(g):
        @pl.when(down4)
        def _():
            in_z(g, 1).wait_recv()

        @pl.when(down8)
        def _():
            in_z(g, 2).wait_recv()

        in_x(g, 0).start()
        in_x(g, 1).start()

    def start_sib(g):
        in_x(g, 0).wait_recv()
        in_x(g, 1).wait_recv()
        in_sib(g).start()

    def back_sib(g):
        return pltpu.make_async_remote_copy(
            src_ref=sib_out.at[g],
            dst_ref=sib_in.at[g],
            send_sem=back_send.at[g, 0],
            recv_sem=back_recv.at[g, 0],
            **to(sibling),
        )

    def back_x(g):
        return pltpu.make_async_remote_copy(
            src_ref=x_out.at[g],
            dst_ref=x_in.at[g],
            send_sem=back_send.at[g, 1],
            recv_sem=back_recv.at[g, 1],
            **to(partner),
        )

    def back_z(g, step):
        return pltpu.make_async_remote_copy(
            src_ref=z_out.at[g, step - 1],
            dst_ref=z_in.at[g, step - 1],
            send_sem=back_send.at[g, 1 + step],
            recv_sem=back_recv.at[g, 1 + step],
            **to(rank - 4 * step),
        )

    def stage_sib(g):
        for j in range(4):
            sib_out[g, j, 0:rows, :] = acc_k[EVENS + j].astype(jnp.bfloat16)
            sib_out[g, j, rows:, :] = acc_v[EVENS + j].astype(jnp.bfloat16)
        back_sib(g).start()
        sum_k[...] = acc_k[0:EVENS]
        sum_v[...] = acc_v[0:EVENS]

    def stage_x(g):
        back_sib(g).wait_recv()
        for j in range(4):
            sum_k[core + j] += sib_in[g, j, 0:rows, :].astype(jnp.float32)
            sum_v[core + j] += sib_in[g, j, rows:, :].astype(jnp.float32)
        for half in range(2):
            x_out[g, half, 0:rows, :] = sum_k[1 + 2 * half].astype(jnp.bfloat16)
            x_out[g, half, rows:, :] = sum_v[1 + 2 * half].astype(jnp.bfloat16)
        back_x(g).start()

    def stage_z(g):
        back_x(g).wait_recv()
        for half in range(2):
            slot = 2 * col + 2 * half
            sum_k[slot] += x_in[g, half, 0:rows, :].astype(jnp.float32)
            sum_v[slot] += x_in[g, half, rows:, :].astype(jnp.float32)
        for step, there in ((1, down4), (2, down8)):
            z_out[g, step - 1, 0:rows, :] = sum_k[2 * step].astype(jnp.bfloat16)
            z_out[g, step - 1, rows:, :] = sum_v[2 * step].astype(jnp.bfloat16)

            @pl.when(there)
            def _(step=step):
                back_z(g, step).start()

    def finish(g):
        for step, there in ((1, up4), (2, up8)):

            @pl.when(there)
            def _(step=step):
                back_z(g, step).wait_recv()
                sum_k[0] += z_in[g, step - 1, 0:rows, :].astype(jnp.float32)
                sum_v[0] += z_in[g, step - 1, rows:, :].astype(jnp.float32)

        cols = pl.ds(pl.multiple_of(g * HEAD_DIM, HEAD_DIM), HEAD_DIM)
        dk_ref[:, cols] = (sum_k[0] * scale).astype(jnp.bfloat16)
        dv_ref[:, cols] = sum_v[0].astype(jnp.bfloat16)

    for g in range(KV_HEADS):
        start_z(g)
    start_x(0)
    start_sib(0)
    start_x(1)
    in_sib(0).wait_recv()

    row_no = lax.broadcasted_iota(jnp.int32, (rows, rows), 0)
    col_no = lax.broadcasted_iota(jnp.int32, (rows, rows), 1)
    for slot in range(BLOCKS):
        line = win[0, slot, 2 * rows :, :].astype(jnp.float32)[0:1]
        key_doc = jnp.broadcast_to(line, (rows, rows)).T
        seen = key_doc == own_doc
        if slot == 0:
            seen = seen & (row_no <= col_no)
        bias[slot * rows : (slot + 1) * rows, :] = jnp.where(seen, 0.0, -1e30)

    def step(t, carry):
        g, pair = t // PAIRS, t % PAIRS

        @pl.when((pair == 0) & (g > 0))
        def _():
            in_sib(g).wait_recv()

        @pl.when((pair == 0) & (g < KV_HEADS - 1))
        def _():
            start_sib(g + 1)

        @pl.when((pair == 2) & (g < KV_HEADS - 2))
        def _():
            start_x(g + 2)

        @pl.when(pair == 0)
        def _():
            acc_k[...] = jnp.zeros_like(acc_k)
            acc_v[...] = jnp.zeros_like(acc_v)

        first = pl.ds(pl.multiple_of(t * 2 * HEAD_DIM, HEAD_DIM), HEAD_DIM)
        second = pl.ds(pl.multiple_of(t * 2 * HEAD_DIM + HEAD_DIM, HEAD_DIM), HEAD_DIM)
        q = jnp.concatenate([q_ref[:, first], q_ref[:, second]], axis=0)
        grad = jnp.concatenate([g_ref[:, first], g_ref[:, second]], axis=0)
        out = jnp.concatenate([o_ref[:, first], o_ref[:, second]], axis=0)
        delta = jnp.sum((grad.astype(jnp.float32) * out.astype(jnp.float32)).T, axis=0, keepdims=True)
        keys = win[g, :, 0:rows, :].reshape(span, HEAD_DIM)
        vals = win[g, :, rows : 2 * rows, :].reshape(span, HEAD_DIM)
        nt = (((1,), (1,)), ((), ()))
        scores = lax.dot_general(keys, q, nt, preferred_element_type=jnp.float32)
        mask = bias[...]
        scores = scores + jnp.concatenate([mask, mask], axis=1)
        top = jnp.max(scores, axis=0, keepdims=True)
        raw = jnp.exp2((scores - top) * exp_scale)
        prob = raw * (1.0 / jnp.sum(raw, axis=0, keepdims=True))
        prob_grad = lax.dot_general(vals, grad, nt, preferred_element_type=jnp.float32)
        low = (prob * (prob_grad - delta)).astype(jnp.bfloat16)
        acc_v[...] += jnp.dot(
            prob.astype(jnp.bfloat16), grad, preferred_element_type=jnp.float32
        ).reshape(BLOCKS, rows, HEAD_DIM)
        acc_k[...] += jnp.dot(low, q, preferred_element_type=jnp.float32).reshape(
            BLOCKS, rows, HEAD_DIM
        )
        tn = (((0,), (0,)), ((), ()))
        dq = lax.dot_general(low, keys, tn, preferred_element_type=jnp.float32) * scale
        dq = dq.astype(jnp.bfloat16)
        dq_ref[:, first] = dq[0:rows]
        dq_ref[:, second] = dq[rows:]

        @pl.when((pair == 0) & (g > 0))
        def _():
            stage_x(g - 1)

        @pl.when((pair == 1) & (g > 0))
        def _():
            stage_z(g - 1)

        @pl.when((pair == 3) & (g > 0))
        def _():
            finish(g - 1)

        @pl.when(pair == 3)
        def _():
            stage_sib(g)

        return carry

    lax.fori_loop(0, KV_HEADS * PAIRS, step, 0)
    last = KV_HEADS - 1
    stage_x(last)
    stage_z(last)
    finish(last)
    for g in range(KV_HEADS):
        in_x(g, 0).wait_send()
        in_x(g, 1).wait_send()
        in_sib(g).wait_send()
        back_sib(g).wait_send()
        back_x(g).wait_send()
        for n, there_in, there_out in ((1, up4, down4), (2, up8, down8)):

            @pl.when(there_in)
            def _(g=g, n=n):
                in_z(g, n).wait_send()

            @pl.when(there_out)
            def _(g=g, n=n):
                back_z(g, n).wait_send()


def on_device(queries, keys, values, out_grad, attn_out, doc_ids):
    ranks = lax.axis_size("ctx")
    rows = queries.shape[0]
    bf16, f32 = jnp.bfloat16, jnp.float32
    vmem = pl.BlockSpec(memory_space=pltpu.VMEM)
    block = (rows, HEAD_DIM)
    pair = (2 * rows, HEAD_DIM)
    return pl.pallas_call(
        functools.partial(kernel, ranks),
        out_shape=(
            jax.ShapeDtypeStruct(queries.shape, bf16),
            jax.ShapeDtypeStruct(keys.shape, bf16),
            jax.ShapeDtypeStruct(values.shape, bf16),
        ),
        in_specs=[vmem] * 6,
        out_specs=(vmem,) * 3,
        scratch_shapes=[
            pltpu.VMEM((KV_HEADS, BLOCKS, 2 * rows + DOC_ROWS, HEAD_DIM), bf16),
            pltpu.VMEM((BLOCKS * rows, rows), f32),
            pltpu.VMEM((BLOCKS,) + block, f32),
            pltpu.VMEM((BLOCKS,) + block, f32),
            pltpu.VMEM((EVENS,) + block, f32),
            pltpu.VMEM((EVENS,) + block, f32),
            pltpu.VMEM((KV_HEADS, 4) + pair, bf16),
            pltpu.VMEM((KV_HEADS, 4) + pair, bf16),
            pltpu.VMEM((KV_HEADS, 2) + pair, bf16),
            pltpu.VMEM((KV_HEADS, 2) + pair, bf16),
            pltpu.VMEM((KV_HEADS, 2) + pair, bf16),
            pltpu.VMEM((KV_HEADS, 2) + pair, bf16),
            pltpu.SemaphoreType.DMA((KV_HEADS, 5)),
            pltpu.SemaphoreType.DMA((KV_HEADS, 5)),
            pltpu.SemaphoreType.DMA((KV_HEADS, 4)),
            pltpu.SemaphoreType.DMA((KV_HEADS, 4)),
        ],
        compiler_params=pltpu.CompilerParams(
            collective_id=0, has_side_effects=True, vmem_limit_bytes=48 * 1024 * 1024
        ),
    )(queries, keys, values, out_grad, attn_out, doc_ids.reshape(1, rows))


def solution(mesh):
    spec = P(("groups", "ctx"), None)
    return jax.shard_map(
        on_device,
        mesh=mesh,
        in_specs=(spec,) * 5 + (P(("groups", "ctx")),),
        out_specs=(spec,) * 3,
        check_vma=False,
    )
```

```python
import functools
import math

import jax
import jax.numpy as jnp
from jax import lax
from jax.experimental import pallas as pl
from jax.experimental.pallas import tpu as pltpu
from jax.sharding import PartitionSpec as P

HEAD_DIM = 128
HEADS = 32
KV_HEADS = 4
BLOCKS = 9
EVENS = 5
PAIRS = 4
DOC_ROWS = 16
CHUNK = 3


def to(rank):
    return dict(device_id={"ctx": rank}, device_id_type=pl.DeviceIdType.MESH)


def kernel(
    ranks,
    q_ref,
    k_ref,
    v_ref,
    g_ref,
    o_ref,
    doc_ref,
    dq_ref,
    dk_ref,
    dv_ref,
    win,
    q_buf,
    g_buf,
    o_buf,
    doc_buf,
    scores,
    weights,
    lows,
    bias,
    acc_k,
    acc_v,
    sum_k,
    sum_v,
    sib_out,
    sib_in,
    x_out,
    x_in,
    z_out,
    z_in,
    in_send,
    in_recv,
    back_send,
    back_recv,
    kv_sem,
    row_sem,
):
    rows = q_buf.shape[0]
    span = BLOCKS * rows
    scale = 1.0 / math.sqrt(HEAD_DIM)
    exp_scale = scale * math.log2(math.e)
    rank = lax.axis_index("ctx")
    core = rank % 2
    col = (rank // 2) % 2
    sibling = rank + 1 - 2 * core
    partner = rank + 2 - 4 * col
    up4, down4, down8 = rank + 4 < ranks, rank >= 4, rank >= 8
    middle = up4 & down4

    barrier = pltpu.get_barrier_semaphore()
    for peer in (sibling, partner):
        pl.semaphore_signal(barrier, inc=1, **to(peer))
    for there, peer in ((up4, rank + 4), (down4, rank - 4)):

        @pl.when(there)
        def _(peer=peer):
            pl.semaphore_signal(barrier, inc=1, **to(peer))

    loads = [pltpu.make_async_copy(doc_ref, doc_buf, row_sem.at[3])]
    for g in range(KV_HEADS):
        cols = pl.ds(g * HEAD_DIM, HEAD_DIM)
        for n, src in ((0, k_ref), (1, v_ref)):
            dst = win.at[g, 0, pl.ds(n * rows, rows)]
            loads.append(pltpu.make_async_copy(src.at[:, cols], dst, kv_sem.at[g, n]))
    for n, (src, dst) in enumerate(((q_ref, q_buf), (g_ref, g_buf), (o_ref, o_buf))):
        loads.append(pltpu.make_async_copy(src, dst, row_sem.at[n]))
    for load in loads:
        load.start()

    for g in range(KV_HEADS):
        for slot, there in ((2, down4), (4, down8)):

            @pl.when(jnp.logical_not(there))
            def _(g=g, slot=slot):
                win[g, slot, 0 : 2 * rows, :] = jnp.zeros((2 * rows, HEAD_DIM), jnp.bfloat16)
                if g == 0:
                    win[g, slot, 2 * rows :, :] = jnp.full((DOC_ROWS, HEAD_DIM), -1.0, jnp.bfloat16)

    loads[0].wait()
    own_doc = doc_buf[...].astype(jnp.float32)
    win[0, 0, 2 * rows :, :] = jnp.broadcast_to(own_doc, (DOC_ROWS, rows)).astype(jnp.bfloat16)
    near = [there.astype(jnp.int32) for there in (up4, down4)]
    pl.semaphore_wait(barrier, 2 + sum(near))

    def part(g, slot):
        return win.at[g, slot, pl.ds(0, 2 * rows + (DOC_ROWS if g == 0 else 0))]

    def in_z(g, hop):
        return pltpu.make_async_remote_copy(
            src_ref=part(g, 2 * hop),
            dst_ref=part(g, 2 * hop + 2),
            send_sem=in_send.at[g, hop],
            recv_sem=in_recv.at[g, hop],
            **to(rank + 4),
        )

    def in_x(g, half):
        return pltpu.make_async_remote_copy(
            src_ref=part(g, 2 * col + 2 * half),
            dst_ref=part(g, 1 + 2 * half),
            send_sem=in_send.at[g, 2 + half],
            recv_sem=in_recv.at[g, 2 + half],
            **to(partner),
        )

    def in_sib(g):
        return pltpu.make_async_remote_copy(
            src_ref=part(g, pl.ds(core, 4)),
            dst_ref=part(g, pl.ds(EVENS, 4)),
            send_sem=in_send.at[g, 4],
            recv_sem=in_recv.at[g, 4],
            **to(sibling),
        )

    def send_own(g):
        loads[1 + 2 * g].wait()
        loads[2 + 2 * g].wait()

        @pl.when(up4)
        def _():
            in_z(g, 0).start()

        @pl.when(col == 0)
        def _():
            in_x(g, 0).start()

    def send_four(g):
        @pl.when(down4)
        def _():
            in_z(g, 0).wait_recv()

        @pl.when(middle)
        def _():
            in_z(g, 1).start()

        @pl.when(col == 0)
        def _():
            in_x(g, 1).start()

        @pl.when(col == 1)
        def _():
            in_x(g, 0).start()

    def send_eight(g):
        @pl.when(down8)
        def _():
            in_z(g, 1).wait_recv()

        @pl.when(col == 1)
        def _():
            in_x(g, 1).start()

    def send_sib(g):
        in_x(g, 0).wait_recv()
        in_x(g, 1).wait_recv()
        in_sib(g).start()

    def back_sib(g):
        return pltpu.make_async_remote_copy(
            src_ref=sib_out.at[g],
            dst_ref=sib_in.at[g],
            send_sem=back_send.at[g, 0],
            recv_sem=back_recv.at[g, 0],
            **to(sibling),
        )

    def back_x(g):
        return pltpu.make_async_remote_copy(
            src_ref=x_out.at[g],
            dst_ref=x_in.at[g],
            send_sem=back_send.at[g, 1],
            recv_sem=back_recv.at[g, 1],
            **to(partner),
        )

    def back_z(g, hop):
        return pltpu.make_async_remote_copy(
            src_ref=z_out.at[g, hop],
            dst_ref=z_in.at[g, hop],
            send_sem=back_send.at[g, 2 + hop],
            recv_sem=back_recv.at[g, 2 + hop],
            **to(rank - 4),
        )

    def stage_sib(g):
        for j in range(4):
            sib_out[g, j, 0:rows, :] = acc_k[EVENS + j].astype(jnp.bfloat16)
            sib_out[g, j, rows:, :] = acc_v[EVENS + j].astype(jnp.bfloat16)
        back_sib(g).start()
        sum_k[...] = acc_k[0:EVENS]
        sum_v[...] = acc_v[0:EVENS]

    def stage_x(g):
        back_sib(g).wait_recv()
        for j in range(4):
            sum_k[core + j] += sib_in[g, j, 0:rows, :].astype(jnp.float32)
            sum_v[core + j] += sib_in[g, j, rows:, :].astype(jnp.float32)
        for half in range(2):
            x_out[g, half, 0:rows, :] = sum_k[1 + 2 * half].astype(jnp.bfloat16)
            x_out[g, half, rows:, :] = sum_v[1 + 2 * half].astype(jnp.bfloat16)
        back_x(g).start()

    def stage_z(g):
        back_x(g).wait_recv()
        for half in range(2):
            slot = 2 * col + 2 * half
            sum_k[slot] += x_in[g, half, 0:rows, :].astype(jnp.float32)
            sum_v[slot] += x_in[g, half, rows:, :].astype(jnp.float32)

        @pl.when(down8)
        def _():
            z_out[g, 0, 0:rows, :] = sum_k[4].astype(jnp.bfloat16)
            z_out[g, 0, rows:, :] = sum_v[4].astype(jnp.bfloat16)
            back_z(g, 0).start()

    def stage_four(g):
        @pl.when(middle)
        def _():
            back_z(g, 0).wait_recv()
            sum_k[2] += z_in[g, 0, 0:rows, :].astype(jnp.float32)
            sum_v[2] += z_in[g, 0, rows:, :].astype(jnp.float32)

        @pl.when(down4)
        def _():
            z_out[g, 1, 0:rows, :] = sum_k[2].astype(jnp.bfloat16)
            z_out[g, 1, rows:, :] = sum_v[2].astype(jnp.bfloat16)
            back_z(g, 1).start()

    def finish(g):
        @pl.when(up4)
        def _():
            back_z(g, 1).wait_recv()
            sum_k[0] += z_in[g, 1, 0:rows, :].astype(jnp.float32)
            sum_v[0] += z_in[g, 1, rows:, :].astype(jnp.float32)

        cols = pl.ds(pl.multiple_of(g * HEAD_DIM, HEAD_DIM), HEAD_DIM)
        dk_ref[:, cols] = (sum_k[0] * scale).astype(jnp.bfloat16)
        dv_ref[:, cols] = sum_v[0].astype(jnp.bfloat16)

    send_own(0)
    send_four(0)
    send_own(1)
    send_eight(0)
    send_four(1)
    send_sib(0)
    send_own(2)
    for load in loads[-3:]:
        load.wait()
    in_sib(0).wait_recv()

    row_no = lax.broadcasted_iota(jnp.int32, (rows, rows), 0)
    col_no = lax.broadcasted_iota(jnp.int32, (rows, rows), 1)
    for slot in range(BLOCKS):
        line = win[0, slot, 2 * rows :, :].astype(jnp.float32)[0:1]
        key_doc = jnp.broadcast_to(line, (rows, rows)).T
        seen = key_doc == own_doc
        if slot == 0:
            seen = seen & (row_no <= col_no)
        bias[slot * rows : (slot + 1) * rows, :] = jnp.where(seen, 0.0, -1e30)

    def step(t, carry):
        g, pair = t // PAIRS, t % PAIRS

        def at(now, *todo):
            @pl.when(t == now)
            def _():
                for call, head in todo:
                    call(head)

        def wait_sib(head):
            in_sib(head).wait_recv()

        at(0, (send_eight, 1), (send_four, 2), (send_own, 3))
        at(1, (send_sib, 1))
        at(2, (send_eight, 2), (send_four, 3))
        at(3, (send_sib, 2))
        at(4, (wait_sib, 1), (send_eight, 3))
        at(5, (send_sib, 3))
        at(8, (wait_sib, 2))
        at(12, (wait_sib, 3))

        @pl.when(pair == 0)
        def _():
            acc_k[...] = jnp.zeros_like(acc_k)
            acc_v[...] = jnp.zeros_like(acc_v)

        first = pl.ds(pl.multiple_of(t * 2 * HEAD_DIM, HEAD_DIM), HEAD_DIM)
        second = pl.ds(pl.multiple_of(t * 2 * HEAD_DIM + HEAD_DIM, HEAD_DIM), HEAD_DIM)
        q = jnp.concatenate([q_buf[:, first], q_buf[:, second]], axis=0)
        grad = jnp.concatenate([g_buf[:, first], g_buf[:, second]], axis=0).astype(jnp.float32)
        out = jnp.concatenate([o_buf[:, first], o_buf[:, second]], axis=0).astype(jnp.float32)
        delta = jnp.sum((grad * out).T, axis=0, keepdims=True)
        nt = (((1,), (1,)), ((), ()))
        tn = (((0,), (0,)), ((), ()))
        top = None
        for c in range(0, BLOCKS, CHUNK):
            keys = win[g, c : c + CHUNK, 0:rows, :].reshape(CHUNK * rows, HEAD_DIM)
            mask = bias[c * rows : (c + CHUNK) * rows, :]
            piece = lax.dot_general(keys, q, nt, preferred_element_type=jnp.float32)
            piece = piece + jnp.concatenate([mask, mask], axis=1)
            scores[c * rows : (c + CHUNK) * rows, :] = piece
            high = jnp.max(piece.reshape(-1, 8, 2 * rows), axis=0)
            top = high if top is None else jnp.maximum(top, high)
        top = jnp.max(top, axis=0, keepdims=True)
        total = None
        for c in range(BLOCKS):
            piece = jnp.exp2((scores[c * rows : (c + 1) * rows, :] - top) * exp_scale)
            weights[c * rows : (c + 1) * rows, :] = piece.astype(jnp.bfloat16)
            more = jnp.sum(piece.reshape(-1, 8, 2 * rows), axis=0)
            total = more if total is None else total + more
        inverse = 1.0 / jnp.sum(total, axis=0, keepdims=True)
        delta = delta * inverse
        grad = (grad * jnp.broadcast_to(inverse, (HEAD_DIM, 2 * rows)).T).astype(jnp.bfloat16)
        for c in range(0, BLOCKS, CHUNK):
            vals = win[g, c : c + CHUNK, rows : 2 * rows, :].reshape(CHUNK * rows, HEAD_DIM)
            piece = lax.dot_general(vals, grad, nt, preferred_element_type=jnp.float32)
            held = weights[c * rows : (c + CHUNK) * rows, :].astype(jnp.float32)
            lows[c * rows : (c + CHUNK) * rows, :] = (held * (piece - delta)).astype(jnp.bfloat16)
        for c in range(0, BLOCKS, CHUNK):
            here = slice(c * rows, (c + CHUNK) * rows)
            acc_v[c : c + CHUNK] += jnp.dot(
                weights[here, :], grad, preferred_element_type=jnp.float32
            ).reshape(CHUNK, rows, HEAD_DIM)
            acc_k[c : c + CHUNK] += jnp.dot(
                lows[here, :], q, preferred_element_type=jnp.float32
            ).reshape(CHUNK, rows, HEAD_DIM)
        keys = win[g, :, 0:rows, :].reshape(span, HEAD_DIM)
        dq = lax.dot_general(lows[...], keys, tn, preferred_element_type=jnp.float32) * scale
        dq = dq.astype(jnp.bfloat16)
        dq_ref[:, first] = dq[0:rows]
        dq_ref[:, second] = dq[rows:]

        @pl.when((pair == 0) & (g > 0))
        def _():
            stage_x(g - 1)

        @pl.when((pair == 1) & (g > 0))
        def _():
            stage_z(g - 1)

        @pl.when((pair == 2) & (g > 0))
        def _():
            stage_four(g - 1)

        @pl.when((pair == 3) & (g > 0))
        def _():
            finish(g - 1)

        @pl.when(pair == 3)
        def _():
            stage_sib(g)

        return carry

    lax.fori_loop(0, KV_HEADS * PAIRS, step, 0)
    last = KV_HEADS - 1
    stage_x(last)
    stage_z(last)
    stage_four(last)
    finish(last)
    for g in range(KV_HEADS):
        in_x(g, 0).wait_send()
        in_x(g, 1).wait_send()
        in_sib(g).wait_send()
        back_sib(g).wait_send()
        back_x(g).wait_send()
        for hop, there_in, there_out in ((0, up4, down8), (1, middle, down4)):

            @pl.when(there_in)
            def _(g=g, hop=hop):
                in_z(g, hop).wait_send()

            @pl.when(there_out)
            def _(g=g, hop=hop):
                back_z(g, hop).wait_send()


def on_device(queries, keys, values, out_grad, attn_out, doc_ids):
    ranks = lax.axis_size("ctx")
    rows = queries.shape[0]
    bf16, f32 = jnp.bfloat16, jnp.float32
    vmem = pl.BlockSpec(memory_space=pltpu.VMEM)
    block = (rows, HEAD_DIM)
    pair = (2 * rows, HEAD_DIM)
    return pl.pallas_call(
        functools.partial(kernel, ranks),
        out_shape=(
            jax.ShapeDtypeStruct(queries.shape, bf16),
            jax.ShapeDtypeStruct(keys.shape, bf16),
            jax.ShapeDtypeStruct(values.shape, bf16),
        ),
        in_specs=[pl.BlockSpec(memory_space=pl.ANY)] * 6,
        out_specs=(vmem,) * 3,
        scratch_shapes=[
            pltpu.VMEM((KV_HEADS, BLOCKS, 2 * rows + DOC_ROWS, HEAD_DIM), bf16),
            pltpu.VMEM(queries.shape, bf16),
            pltpu.VMEM(queries.shape, bf16),
            pltpu.VMEM(queries.shape, bf16),
            pltpu.VMEM((1, rows), jnp.int32),
            pltpu.VMEM((BLOCKS * rows, 2 * rows), f32),
            pltpu.VMEM((BLOCKS * rows, 2 * rows), bf16),
            pltpu.VMEM((BLOCKS * rows, 2 * rows), bf16),
            pltpu.VMEM((BLOCKS * rows, rows), f32),
            pltpu.VMEM((BLOCKS,) + block, f32),
            pltpu.VMEM((BLOCKS,) + block, f32),
            pltpu.VMEM((EVENS,) + block, f32),
            pltpu.VMEM((EVENS,) + block, f32),
            pltpu.VMEM((KV_HEADS, 4) + pair, bf16),
            pltpu.VMEM((KV_HEADS, 4) + pair, bf16),
            pltpu.VMEM((KV_HEADS, 2) + pair, bf16),
            pltpu.VMEM((KV_HEADS, 2) + pair, bf16),
            pltpu.VMEM((KV_HEADS, 2) + pair, bf16),
            pltpu.VMEM((KV_HEADS, 2) + pair, bf16),
            pltpu.SemaphoreType.DMA((KV_HEADS, 5)),
            pltpu.SemaphoreType.DMA((KV_HEADS, 5)),
            pltpu.SemaphoreType.DMA((KV_HEADS, 4)),
            pltpu.SemaphoreType.DMA((KV_HEADS, 4)),
            pltpu.SemaphoreType.DMA((KV_HEADS, 2)),
            pltpu.SemaphoreType.DMA((4,)),
        ],
        compiler_params=pltpu.CompilerParams(
            collective_id=0, has_side_effects=True, vmem_limit_bytes=48 * 1024 * 1024
        ),
    )(queries, keys, values, out_grad, attn_out, doc_ids.reshape(1, rows))


def solution(mesh):
    spec = P(("groups", "ctx"), None)
    return jax.shard_map(
        on_device,
        mesh=mesh,
        in_specs=(spec,) * 5 + (P(("groups", "ctx")),),
        out_specs=(spec,) * 3,
        check_vma=False,
    )
```

```python
import functools
import math

import jax
import jax.numpy as jnp
from jax import lax
from jax.experimental import pallas as pl
from jax.experimental.pallas import tpu as pltpu
from jax.sharding import PartitionSpec as P

HEAD_DIM = 128
HEADS = 32
KV_HEADS = 4
BLOCKS = 9
EVENS = 5
PAIRS = 4
DOC_ROWS = 16
CHUNK = 3


def to(rank):
    return dict(device_id={"ctx": rank}, device_id_type=pl.DeviceIdType.MESH)


def kernel(
    ranks,
    q_ref,
    k_ref,
    v_ref,
    g_ref,
    o_ref,
    doc_ref,
    dq_ref,
    dk_ref,
    dv_ref,
    win,
    q_buf,
    g_buf,
    o_buf,
    doc_buf,
    scores,
    weights,
    lows,
    bias,
    acc_k,
    acc_v,
    sum_k,
    sum_v,
    sib_out,
    sib_in,
    x_out,
    x_in,
    z_out,
    z_in,
    in_send,
    in_recv,
    back_send,
    back_recv,
    kv_sem,
    row_sem,
):
    rows = q_buf.shape[0]
    span = BLOCKS * rows
    scale = 1.0 / math.sqrt(HEAD_DIM)
    exp_scale = scale * math.log2(math.e)
    rank = lax.axis_index("ctx")
    core = rank % 2
    col = (rank // 2) % 2
    sibling = rank + 1 - 2 * core
    partner = rank + 2 - 4 * col
    up4, down4, down8 = rank + 4 < ranks, rank >= 4, rank >= 8
    middle = up4 & down4

    barrier = pltpu.get_barrier_semaphore()
    for peer in (sibling, partner):
        pl.semaphore_signal(barrier, inc=1, **to(peer))
    for there, peer in ((up4, rank + 4), (down4, rank - 4)):

        @pl.when(there)
        def _(peer=peer):
            pl.semaphore_signal(barrier, inc=1, **to(peer))

    loads = [pltpu.make_async_copy(doc_ref, doc_buf, row_sem.at[3])]
    for g in range(KV_HEADS):
        cols = pl.ds(g * HEAD_DIM, HEAD_DIM)
        for n, src in ((0, k_ref), (1, v_ref)):
            dst = win.at[g, 0, pl.ds(n * rows, rows)]
            loads.append(pltpu.make_async_copy(src.at[:, cols], dst, kv_sem.at[g, n]))
    for n, (src, dst) in enumerate(((q_ref, q_buf), (g_ref, g_buf), (o_ref, o_buf))):
        loads.append(pltpu.make_async_copy(src, dst, row_sem.at[n]))
    for load in loads:
        load.start()

    for g in range(KV_HEADS):
        for slot, there in ((2, down4), (4, down8)):

            @pl.when(jnp.logical_not(there))
            def _(g=g, slot=slot):
                win[g, slot, 0 : 2 * rows, :] = jnp.zeros((2 * rows, HEAD_DIM), jnp.bfloat16)
                if g == 0:
                    win[g, slot, 2 * rows :, :] = jnp.full((DOC_ROWS, HEAD_DIM), -1.0, jnp.bfloat16)

    loads[0].wait()
    own_doc = doc_buf[...].astype(jnp.float32)
    win[0, 0, 2 * rows :, :] = jnp.broadcast_to(own_doc, (DOC_ROWS, rows)).astype(jnp.bfloat16)
    near = [there.astype(jnp.int32) for there in (up4, down4)]
    pl.semaphore_wait(barrier, 2 + sum(near))

    def part(g, slot):
        return win.at[g, slot, pl.ds(0, 2 * rows + (DOC_ROWS if g == 0 else 0))]

    def in_z(g, hop):
        return pltpu.make_async_remote_copy(
            src_ref=part(g, 2 * hop),
            dst_ref=part(g, 2 * hop + 2),
            send_sem=in_send.at[g, hop],
            recv_sem=in_recv.at[g, hop],
            **to(rank + 4),
        )

    def in_x(g, half):
        return pltpu.make_async_remote_copy(
            src_ref=part(g, 2 * col + 2 * half),
            dst_ref=part(g, 1 + 2 * half),
            send_sem=in_send.at[g, 2 + half],
            recv_sem=in_recv.at[g, 2 + half],
            **to(partner),
        )

    def in_sib(g):
        return pltpu.make_async_remote_copy(
            src_ref=part(g, pl.ds(core, 4)),
            dst_ref=part(g, pl.ds(EVENS, 4)),
            send_sem=in_send.at[g, 4],
            recv_sem=in_recv.at[g, 4],
            **to(sibling),
        )

    def send_own(g):
        loads[1 + 2 * g].wait()
        loads[2 + 2 * g].wait()

        @pl.when(up4)
        def _():
            in_z(g, 0).start()

        @pl.when(col == 0)
        def _():
            in_x(g, 0).start()

    def send_four(g):
        @pl.when(down4)
        def _():
            in_z(g, 0).wait_recv()

        @pl.when(middle)
        def _():
            in_z(g, 1).start()

        @pl.when(col == 0)
        def _():
            in_x(g, 1).start()

        @pl.when(col == 1)
        def _():
            in_x(g, 0).start()

    def send_eight(g):
        @pl.when(down8)
        def _():
            in_z(g, 1).wait_recv()

        @pl.when(col == 1)
        def _():
            in_x(g, 1).start()

    def send_sib(g):
        in_x(g, 0).wait_recv()
        in_x(g, 1).wait_recv()
        in_sib(g).start()

    def back_sib(g):
        return pltpu.make_async_remote_copy(
            src_ref=sib_out.at[g],
            dst_ref=sib_in.at[g],
            send_sem=back_send.at[g, 0],
            recv_sem=back_recv.at[g, 0],
            **to(sibling),
        )

    def back_x(g):
        return pltpu.make_async_remote_copy(
            src_ref=x_out.at[g],
            dst_ref=x_in.at[g],
            send_sem=back_send.at[g, 1],
            recv_sem=back_recv.at[g, 1],
            **to(partner),
        )

    def back_z(g, hop):
        return pltpu.make_async_remote_copy(
            src_ref=z_out.at[g, hop],
            dst_ref=z_in.at[g, hop],
            send_sem=back_send.at[g, 2 + hop],
            recv_sem=back_recv.at[g, 2 + hop],
            **to(rank - 4),
        )

    def stage_sib(g):
        for j in range(4):
            sib_out[g, j, 0:rows, :] = acc_k[EVENS + j].astype(jnp.bfloat16)
            sib_out[g, j, rows:, :] = acc_v[EVENS + j].astype(jnp.bfloat16)
        back_sib(g).start()
        sum_k[g % 2] = acc_k[0:EVENS]
        sum_v[g % 2] = acc_v[0:EVENS]

    def stage_x(g):
        back_sib(g).wait_recv()
        for j in range(4):
            sum_k[g % 2, core + j] += sib_in[g, j, 0:rows, :].astype(jnp.float32)
            sum_v[g % 2, core + j] += sib_in[g, j, rows:, :].astype(jnp.float32)
        for half in range(2):
            x_out[g, half, 0:rows, :] = sum_k[g % 2, 1 + 2 * half].astype(jnp.bfloat16)
            x_out[g, half, rows:, :] = sum_v[g % 2, 1 + 2 * half].astype(jnp.bfloat16)
        back_x(g).start()

    def stage_z(g):
        back_x(g).wait_recv()
        for half in range(2):
            slot = 2 * col + 2 * half
            sum_k[g % 2, slot] += x_in[g, half, 0:rows, :].astype(jnp.float32)
            sum_v[g % 2, slot] += x_in[g, half, rows:, :].astype(jnp.float32)

        @pl.when(down8)
        def _():
            z_out[g, 0, 0:rows, :] = sum_k[g % 2, 4].astype(jnp.bfloat16)
            z_out[g, 0, rows:, :] = sum_v[g % 2, 4].astype(jnp.bfloat16)
            back_z(g, 0).start()

    def stage_four(g):
        @pl.when(middle)
        def _():
            back_z(g, 0).wait_recv()
            sum_k[g % 2, 2] += z_in[g, 0, 0:rows, :].astype(jnp.float32)
            sum_v[g % 2, 2] += z_in[g, 0, rows:, :].astype(jnp.float32)

        @pl.when(down4)
        def _():
            z_out[g, 1, 0:rows, :] = sum_k[g % 2, 2].astype(jnp.bfloat16)
            z_out[g, 1, rows:, :] = sum_v[g % 2, 2].astype(jnp.bfloat16)
            back_z(g, 1).start()

    def finish(g):
        @pl.when(up4)
        def _():
            back_z(g, 1).wait_recv()
            sum_k[g % 2, 0] += z_in[g, 1, 0:rows, :].astype(jnp.float32)
            sum_v[g % 2, 0] += z_in[g, 1, rows:, :].astype(jnp.float32)

        cols = pl.ds(pl.multiple_of(g * HEAD_DIM, HEAD_DIM), HEAD_DIM)
        dk_ref[:, cols] = (sum_k[g % 2, 0] * scale).astype(jnp.bfloat16)
        dv_ref[:, cols] = sum_v[g % 2, 0].astype(jnp.bfloat16)

    send_own(0)
    send_four(0)
    send_own(1)
    send_eight(0)
    send_four(1)
    send_sib(0)
    send_own(2)
    for load in loads[-3:]:
        load.wait()
    in_sib(0).wait_recv()

    row_no = lax.broadcasted_iota(jnp.int32, (rows, rows), 0)
    col_no = lax.broadcasted_iota(jnp.int32, (rows, rows), 1)
    for slot in range(BLOCKS):
        line = win[0, slot, 2 * rows :, :].astype(jnp.float32)[0:1]
        key_doc = jnp.broadcast_to(line, (rows, rows)).T
        seen = key_doc == own_doc
        if slot == 0:
            seen = seen & (row_no <= col_no)
        bias[slot * rows : (slot + 1) * rows, :] = jnp.where(seen, 0.0, -1e30)

    def step(t, carry):
        g, pair = t // PAIRS, t % PAIRS

        def at(now, *todo):
            @pl.when(t == now)
            def _():
                for call, head in todo:
                    call(head)

        def wait_sib(head):
            in_sib(head).wait_recv()

        at(0, (send_eight, 1), (send_four, 2), (send_own, 3))
        at(1, (send_sib, 1))
        at(2, (send_eight, 2), (send_four, 3))
        at(3, (send_sib, 2))
        at(4, (wait_sib, 1), (send_eight, 3))
        at(5, (send_sib, 3))
        at(8, (wait_sib, 2))
        at(12, (wait_sib, 3))

        @pl.when(pair == 0)
        def _():
            acc_k[...] = jnp.zeros_like(acc_k)
            acc_v[...] = jnp.zeros_like(acc_v)

        first = pl.ds(pl.multiple_of(t * 2 * HEAD_DIM, HEAD_DIM), HEAD_DIM)
        second = pl.ds(pl.multiple_of(t * 2 * HEAD_DIM + HEAD_DIM, HEAD_DIM), HEAD_DIM)
        q = jnp.concatenate([q_buf[:, first], q_buf[:, second]], axis=0)
        grad = jnp.concatenate([g_buf[:, first], g_buf[:, second]], axis=0).astype(jnp.float32)
        out = jnp.concatenate([o_buf[:, first], o_buf[:, second]], axis=0).astype(jnp.float32)
        delta = jnp.sum((grad * out).T, axis=0, keepdims=True)
        nt = (((1,), (1,)), ((), ()))
        tn = (((0,), (0,)), ((), ()))
        top = None
        for c in range(0, BLOCKS, CHUNK):
            keys = win[g, c : c + CHUNK, 0:rows, :].reshape(CHUNK * rows, HEAD_DIM)
            mask = bias[c * rows : (c + CHUNK) * rows, :]
            piece = lax.dot_general(keys, q, nt, preferred_element_type=jnp.float32)
            piece = piece + jnp.concatenate([mask, mask], axis=1)
            scores[c * rows : (c + CHUNK) * rows, :] = piece
            high = jnp.max(piece.reshape(-1, 8, 2 * rows), axis=0)
            top = high if top is None else jnp.maximum(top, high)
        top = jnp.max(top, axis=0, keepdims=True)
        total = None
        for c in range(BLOCKS):
            piece = jnp.exp2((scores[c * rows : (c + 1) * rows, :] - top) * exp_scale)
            weights[c * rows : (c + 1) * rows, :] = piece.astype(jnp.bfloat16)
            more = jnp.sum(piece.reshape(-1, 8, 2 * rows), axis=0)
            total = more if total is None else total + more
        inverse = 1.0 / jnp.sum(total, axis=0, keepdims=True)
        delta = delta * inverse
        grad = (grad * jnp.broadcast_to(inverse, (HEAD_DIM, 2 * rows)).T).astype(jnp.bfloat16)
        for c in range(0, BLOCKS, CHUNK):
            vals = win[g, c : c + CHUNK, rows : 2 * rows, :].reshape(CHUNK * rows, HEAD_DIM)
            piece = lax.dot_general(vals, grad, nt, preferred_element_type=jnp.float32)
            held = weights[c * rows : (c + CHUNK) * rows, :].astype(jnp.float32)
            lows[c * rows : (c + CHUNK) * rows, :] = (held * (piece - delta)).astype(jnp.bfloat16)
        for c in range(0, BLOCKS, CHUNK):
            here = slice(c * rows, (c + CHUNK) * rows)
            acc_v[c : c + CHUNK] += jnp.dot(
                weights[here, :], grad, preferred_element_type=jnp.float32
            ).reshape(CHUNK, rows, HEAD_DIM)
            acc_k[c : c + CHUNK] += jnp.dot(
                lows[here, :], q, preferred_element_type=jnp.float32
            ).reshape(CHUNK, rows, HEAD_DIM)
        keys = win[g, :, 0:rows, :].reshape(span, HEAD_DIM)
        dq = lax.dot_general(lows[...], keys, tn, preferred_element_type=jnp.float32) * scale
        dq = dq.astype(jnp.bfloat16)
        dq_ref[:, first] = dq[0:rows]
        dq_ref[:, second] = dq[rows:]

        at(5, (stage_x, 0))
        at(8, (stage_z, 0))
        at(9, (stage_x, 1), (stage_four, 0))
        at(11, (finish, 0))
        at(12, (stage_z, 1))
        at(13, (stage_x, 2), (stage_four, 1))
        at(15, (finish, 1), (stage_z, 2))

        @pl.when(pair == 3)
        def _():
            stage_sib(g)

        return carry

    lax.fori_loop(0, KV_HEADS * PAIRS, step, 0)
    last = KV_HEADS - 1
    stage_x(last)
    stage_four(last - 1)
    stage_z(last)
    finish(last - 1)
    stage_four(last)
    finish(last)
    for g in range(KV_HEADS):
        in_x(g, 0).wait_send()
        in_x(g, 1).wait_send()
        in_sib(g).wait_send()
        back_sib(g).wait_send()
        back_x(g).wait_send()
        for hop, there_in, there_out in ((0, up4, down8), (1, middle, down4)):

            @pl.when(there_in)
            def _(g=g, hop=hop):
                in_z(g, hop).wait_send()

            @pl.when(there_out)
            def _(g=g, hop=hop):
                back_z(g, hop).wait_send()


def on_device(queries, keys, values, out_grad, attn_out, doc_ids):
    ranks = lax.axis_size("ctx")
    rows = queries.shape[0]
    bf16, f32 = jnp.bfloat16, jnp.float32
    vmem = pl.BlockSpec(memory_space=pltpu.VMEM)
    block = (rows, HEAD_DIM)
    pair = (2 * rows, HEAD_DIM)
    return pl.pallas_call(
        functools.partial(kernel, ranks),
        out_shape=(
            jax.ShapeDtypeStruct(queries.shape, bf16),
            jax.ShapeDtypeStruct(keys.shape, bf16),
            jax.ShapeDtypeStruct(values.shape, bf16),
        ),
        in_specs=[pl.BlockSpec(memory_space=pl.ANY)] * 6,
        out_specs=(vmem,) * 3,
        scratch_shapes=[
            pltpu.VMEM((KV_HEADS, BLOCKS, 2 * rows + DOC_ROWS, HEAD_DIM), bf16),
            pltpu.VMEM(queries.shape, bf16),
            pltpu.VMEM(queries.shape, bf16),
            pltpu.VMEM(queries.shape, bf16),
            pltpu.VMEM((1, rows), jnp.int32),
            pltpu.VMEM((BLOCKS * rows, 2 * rows), f32),
            pltpu.VMEM((BLOCKS * rows, 2 * rows), bf16),
            pltpu.VMEM((BLOCKS * rows, 2 * rows), bf16),
            pltpu.VMEM((BLOCKS * rows, rows), f32),
            pltpu.VMEM((BLOCKS,) + block, f32),
            pltpu.VMEM((BLOCKS,) + block, f32),
            pltpu.VMEM((2, EVENS) + block, f32),
            pltpu.VMEM((2, EVENS) + block, f32),
            pltpu.VMEM((KV_HEADS, 4) + pair, bf16),
            pltpu.VMEM((KV_HEADS, 4) + pair, bf16),
            pltpu.VMEM((KV_HEADS, 2) + pair, bf16),
            pltpu.VMEM((KV_HEADS, 2) + pair, bf16),
            pltpu.VMEM((KV_HEADS, 2) + pair, bf16),
            pltpu.VMEM((KV_HEADS, 2) + pair, bf16),
            pltpu.SemaphoreType.DMA((KV_HEADS, 5)),
            pltpu.SemaphoreType.DMA((KV_HEADS, 5)),
            pltpu.SemaphoreType.DMA((KV_HEADS, 4)),
            pltpu.SemaphoreType.DMA((KV_HEADS, 4)),
            pltpu.SemaphoreType.DMA((KV_HEADS, 2)),
            pltpu.SemaphoreType.DMA((4,)),
        ],
        compiler_params=pltpu.CompilerParams(
            collective_id=0, has_side_effects=True, vmem_limit_bytes=48 * 1024 * 1024
        ),
    )(queries, keys, values, out_grad, attn_out, doc_ids.reshape(1, rows))


def solution(mesh):
    spec = P(("groups", "ctx"), None)
    return jax.shard_map(
        on_device,
        mesh=mesh,
        in_specs=(spec,) * 5 + (P(("groups", "ctx")),),
        out_specs=(spec,) * 3,
        check_vma=False,
    )
```

```python
import functools
import math

import jax
import jax.numpy as jnp
from jax import lax
from jax.experimental import pallas as pl
from jax.experimental.pallas import tpu as pltpu
from jax.sharding import PartitionSpec as P

HEAD_DIM = 128
HEADS = 32
KV_HEADS = 4
BLOCKS = 9
EVENS = 5
PAIRS = 4
DOC_ROWS = 16
CHUNK = 3


def to(rank):
    return dict(device_id={"ctx": rank}, device_id_type=pl.DeviceIdType.MESH)


def kernel(
    ranks,
    q_ref,
    k_ref,
    v_ref,
    g_ref,
    o_ref,
    doc_ref,
    dq_ref,
    dk_ref,
    dv_ref,
    win,
    q_buf,
    g_buf,
    o_buf,
    doc_buf,
    scores,
    weights,
    lows,
    bias,
    acc_k,
    acc_v,
    sum_k,
    sum_v,
    sib_out,
    sib_in,
    x_out,
    x_in,
    z_out,
    z_in,
    in_send,
    in_recv,
    back_send,
    back_recv,
    kv_sem,
    row_sem,
):
    rows = q_buf.shape[0]
    span = BLOCKS * rows
    scale = 1.0 / math.sqrt(HEAD_DIM)
    exp_scale = scale * math.log2(math.e)
    rank = lax.axis_index("ctx")
    core = rank % 2
    col = (rank // 2) % 2
    sibling = rank + 1 - 2 * core
    partner = rank + 2 - 4 * col
    up4, down4, down8 = rank + 4 < ranks, rank >= 4, rank >= 8
    middle = up4 & down4

    barrier = pltpu.get_barrier_semaphore()
    for peer in (sibling, partner):
        pl.semaphore_signal(barrier, inc=1, **to(peer))
    for there, peer in ((up4, rank + 4), (down4, rank - 4)):

        @pl.when(there)
        def _(peer=peer):
            pl.semaphore_signal(barrier, inc=1, **to(peer))

    loads = [pltpu.make_async_copy(doc_ref, doc_buf, row_sem.at[3])]
    for g in range(KV_HEADS):
        cols = pl.ds(g * HEAD_DIM, HEAD_DIM)
        for n, src in ((0, k_ref), (1, v_ref)):
            dst = win.at[g, 0, pl.ds(n * rows, rows)]
            loads.append(pltpu.make_async_copy(src.at[:, cols], dst, kv_sem.at[g, n]))
    for n, (src, dst) in enumerate(((q_ref, q_buf), (g_ref, g_buf), (o_ref, o_buf))):
        loads.append(pltpu.make_async_copy(src, dst, row_sem.at[n]))
    for load in loads:
        load.start()

    for g in range(KV_HEADS):
        for slot, there in ((2, down4), (4, down8)):

            @pl.when(jnp.logical_not(there))
            def _(g=g, slot=slot):
                win[g, slot, 0 : 2 * rows, :] = jnp.zeros((2 * rows, HEAD_DIM), jnp.bfloat16)
                if g == 0:
                    win[g, slot, 2 * rows :, :] = jnp.full((DOC_ROWS, HEAD_DIM), -1.0, jnp.bfloat16)

    loads[0].wait()
    own_doc = doc_buf[...].astype(jnp.float32)
    win[0, 0, 2 * rows :, :] = jnp.broadcast_to(own_doc, (DOC_ROWS, rows)).astype(jnp.bfloat16)
    near = [there.astype(jnp.int32) for there in (up4, down4)]
    pl.semaphore_wait(barrier, 2 + sum(near))

    def part(g, slot):
        return win.at[g, slot, pl.ds(0, 2 * rows + (DOC_ROWS if g == 0 else 0))]

    def in_z(g, hop):
        return pltpu.make_async_remote_copy(
            src_ref=part(g, 2 * hop),
            dst_ref=part(g, 2 * hop + 2),
            send_sem=in_send.at[g, hop],
            recv_sem=in_recv.at[g, hop],
            **to(rank + 4),
        )

    def in_x(g, half):
        return pltpu.make_async_remote_copy(
            src_ref=part(g, 2 * col + 2 * half),
            dst_ref=part(g, 1 + 2 * half),
            send_sem=in_send.at[g, 2 + half],
            recv_sem=in_recv.at[g, 2 + half],
            **to(partner),
        )

    def in_sib(g, half):
        return pltpu.make_async_remote_copy(
            src_ref=part(g, pl.ds(core + 2 * half, 2)),
            dst_ref=part(g, pl.ds(EVENS + 2 * half, 2)),
            send_sem=in_send.at[g, 4 + half],
            recv_sem=in_recv.at[g, 4 + half],
            **to(sibling),
        )

    def send_own(g):
        loads[1 + 2 * g].wait()
        loads[2 + 2 * g].wait()

        @pl.when(up4)
        def _():
            in_z(g, 0).start()

        @pl.when(col == 0)
        def _():
            in_x(g, 0).start()

    def send_four(g):
        @pl.when(down4)
        def _():
            in_z(g, 0).wait_recv()

        @pl.when(middle)
        def _():
            in_z(g, 1).start()

        @pl.when(col == 0)
        def _():
            in_x(g, 1).start()

        @pl.when(col == 1)
        def _():
            in_x(g, 0).start()

    def send_eight(g):
        @pl.when(down8)
        def _():
            in_z(g, 1).wait_recv()

        @pl.when(col == 1)
        def _():
            in_x(g, 1).start()

    def send_sib(g):
        in_x(g, 0).wait_recv()
        in_sib(g, 0).start()
        in_x(g, 1).wait_recv()
        in_sib(g, 1).start()

    def back_sib(g):
        return pltpu.make_async_remote_copy(
            src_ref=sib_out.at[g],
            dst_ref=sib_in.at[g],
            send_sem=back_send.at[g, 0],
            recv_sem=back_recv.at[g, 0],
            **to(sibling),
        )

    def back_x(g):
        return pltpu.make_async_remote_copy(
            src_ref=x_out.at[g],
            dst_ref=x_in.at[g],
            send_sem=back_send.at[g, 1],
            recv_sem=back_recv.at[g, 1],
            **to(partner),
        )

    def back_z(g, hop):
        return pltpu.make_async_remote_copy(
            src_ref=z_out.at[g, hop],
            dst_ref=z_in.at[g, hop],
            send_sem=back_send.at[g, 2 + hop],
            recv_sem=back_recv.at[g, 2 + hop],
            **to(rank - 4),
        )

    def stage_sib(g):
        for j in range(4):
            sib_out[g, j, 0:rows, :] = acc_k[EVENS + j].astype(jnp.bfloat16)
            sib_out[g, j, rows:, :] = acc_v[EVENS + j].astype(jnp.bfloat16)
        back_sib(g).start()
        sum_k[g % 2] = acc_k[0:EVENS]
        sum_v[g % 2] = acc_v[0:EVENS]

    def stage_x(g):
        back_sib(g).wait_recv()
        for j in range(4):
            sum_k[g % 2, core + j] += sib_in[g, j, 0:rows, :].astype(jnp.float32)
            sum_v[g % 2, core + j] += sib_in[g, j, rows:, :].astype(jnp.float32)
        for half in range(2):
            x_out[g, half, 0:rows, :] = sum_k[g % 2, 1 + 2 * half].astype(jnp.bfloat16)
            x_out[g, half, rows:, :] = sum_v[g % 2, 1 + 2 * half].astype(jnp.bfloat16)
        back_x(g).start()

    def stage_z(g):
        back_x(g).wait_recv()
        for half in range(2):
            slot = 2 * col + 2 * half
            sum_k[g % 2, slot] += x_in[g, half, 0:rows, :].astype(jnp.float32)
            sum_v[g % 2, slot] += x_in[g, half, rows:, :].astype(jnp.float32)

        @pl.when(down8)
        def _():
            z_out[g, 0, 0:rows, :] = sum_k[g % 2, 4].astype(jnp.bfloat16)
            z_out[g, 0, rows:, :] = sum_v[g % 2, 4].astype(jnp.bfloat16)
            back_z(g, 0).start()

    def stage_four(g):
        @pl.when(middle)
        def _():
            back_z(g, 0).wait_recv()
            sum_k[g % 2, 2] += z_in[g, 0, 0:rows, :].astype(jnp.float32)
            sum_v[g % 2, 2] += z_in[g, 0, rows:, :].astype(jnp.float32)

        @pl.when(down4)
        def _():
            z_out[g, 1, 0:rows, :] = sum_k[g % 2, 2].astype(jnp.bfloat16)
            z_out[g, 1, rows:, :] = sum_v[g % 2, 2].astype(jnp.bfloat16)
            back_z(g, 1).start()

    def finish(g):
        @pl.when(up4)
        def _():
            back_z(g, 1).wait_recv()
            sum_k[g % 2, 0] += z_in[g, 1, 0:rows, :].astype(jnp.float32)
            sum_v[g % 2, 0] += z_in[g, 1, rows:, :].astype(jnp.float32)

        cols = pl.ds(pl.multiple_of(g * HEAD_DIM, HEAD_DIM), HEAD_DIM)
        dk_ref[:, cols] = (sum_k[g % 2, 0] * scale).astype(jnp.bfloat16)
        dv_ref[:, cols] = sum_v[g % 2, 0].astype(jnp.bfloat16)

    send_own(0)
    send_four(0)
    send_own(1)
    send_eight(0)
    send_four(1)
    send_sib(0)
    send_own(2)
    for load in loads[-3:]:
        load.wait()
    in_sib(0, 0).wait_recv()
    in_sib(0, 1).wait_recv()

    row_no = lax.broadcasted_iota(jnp.int32, (rows, rows), 0)
    col_no = lax.broadcasted_iota(jnp.int32, (rows, rows), 1)
    for slot in range(BLOCKS):
        line = win[0, slot, 2 * rows :, :].astype(jnp.float32)[0:1]
        key_doc = jnp.broadcast_to(line, (rows, rows)).T
        seen = key_doc == own_doc
        if slot == 0:
            seen = seen & (row_no <= col_no)
        bias[slot * rows : (slot + 1) * rows, :] = jnp.where(seen, 0.0, -1e30)

    def step(t, carry):
        g, pair = t // PAIRS, t % PAIRS

        def at(now, *todo):
            @pl.when(t == now)
            def _():
                for call, head in todo:
                    call(head)

        def wait_sib(head):
            in_sib(head, 0).wait_recv()
            in_sib(head, 1).wait_recv()

        at(0, (send_eight, 1), (send_four, 2), (send_own, 3))
        at(1, (send_sib, 1))
        at(2, (send_eight, 2), (send_four, 3))
        at(3, (send_sib, 2))
        at(4, (wait_sib, 1), (send_eight, 3))
        at(5, (send_sib, 3))
        at(8, (wait_sib, 2))
        at(12, (wait_sib, 3))

        @pl.when(pair == 0)
        def _():
            acc_k[...] = jnp.zeros_like(acc_k)
            acc_v[...] = jnp.zeros_like(acc_v)

        first = pl.ds(pl.multiple_of(t * 2 * HEAD_DIM, HEAD_DIM), HEAD_DIM)
        second = pl.ds(pl.multiple_of(t * 2 * HEAD_DIM + HEAD_DIM, HEAD_DIM), HEAD_DIM)
        q = jnp.concatenate([q_buf[:, first], q_buf[:, second]], axis=0)
        grad = jnp.concatenate([g_buf[:, first], g_buf[:, second]], axis=0).astype(jnp.float32)
        out = jnp.concatenate([o_buf[:, first], o_buf[:, second]], axis=0).astype(jnp.float32)
        delta = jnp.sum((grad * out).T, axis=0, keepdims=True)
        nt = (((1,), (1,)), ((), ()))
        tn = (((0,), (0,)), ((), ()))
        top = None
        for c in range(0, BLOCKS, CHUNK):
            keys = win[g, c : c + CHUNK, 0:rows, :].reshape(CHUNK * rows, HEAD_DIM)
            mask = bias[c * rows : (c + CHUNK) * rows, :]
            piece = lax.dot_general(keys, q, nt, preferred_element_type=jnp.float32)
            piece = piece + jnp.concatenate([mask, mask], axis=1)
            scores[c * rows : (c + CHUNK) * rows, :] = piece
            high = jnp.max(piece.reshape(-1, 8, 2 * rows), axis=0)
            top = high if top is None else jnp.maximum(top, high)
        top = jnp.max(top, axis=0, keepdims=True)
        total = None
        for c in range(BLOCKS):
            piece = jnp.exp2((scores[c * rows : (c + 1) * rows, :] - top) * exp_scale)
            weights[c * rows : (c + 1) * rows, :] = piece.astype(jnp.bfloat16)
            more = jnp.sum(piece.reshape(-1, 8, 2 * rows), axis=0)
            total = more if total is None else total + more
        inverse = 1.0 / jnp.sum(total, axis=0, keepdims=True)
        delta = delta * inverse
        grad = (grad * jnp.broadcast_to(inverse, (HEAD_DIM, 2 * rows)).T).astype(jnp.bfloat16)
        for c in range(0, BLOCKS, CHUNK):
            vals = win[g, c : c + CHUNK, rows : 2 * rows, :].reshape(CHUNK * rows, HEAD_DIM)
            piece = lax.dot_general(vals, grad, nt, preferred_element_type=jnp.float32)
            held = weights[c * rows : (c + CHUNK) * rows, :].astype(jnp.float32)
            lows[c * rows : (c + CHUNK) * rows, :] = (held * (piece - delta)).astype(jnp.bfloat16)
        for c in range(0, BLOCKS, CHUNK):
            here = slice(c * rows, (c + CHUNK) * rows)
            acc_v[c : c + CHUNK] += jnp.dot(
                weights[here, :], grad, preferred_element_type=jnp.float32
            ).reshape(CHUNK, rows, HEAD_DIM)
            acc_k[c : c + CHUNK] += jnp.dot(
                lows[here, :], q, preferred_element_type=jnp.float32
            ).reshape(CHUNK, rows, HEAD_DIM)
        keys = win[g, :, 0:rows, :].reshape(span, HEAD_DIM)
        dq = lax.dot_general(lows[...], keys, tn, preferred_element_type=jnp.float32) * scale
        dq = dq.astype(jnp.bfloat16)
        dq_ref[:, first] = dq[0:rows]
        dq_ref[:, second] = dq[rows:]

        at(5, (stage_x, 0))
        at(8, (stage_z, 0))
        at(9, (stage_x, 1), (stage_four, 0))
        at(11, (finish, 0))
        at(12, (stage_z, 1))
        at(13, (stage_x, 2), (stage_four, 1))
        at(15, (finish, 1))

        @pl.when(pair == 3)
        def _():
            stage_sib(g)

        at(15, (stage_z, 2))
        return carry

    lax.fori_loop(0, KV_HEADS * PAIRS, step, 0)
    last = KV_HEADS - 1
    stage_x(last)
    stage_four(last - 1)
    stage_z(last)
    finish(last - 1)
    stage_four(last)
    finish(last)
    for g in range(KV_HEADS):
        in_x(g, 0).wait_send()
        in_x(g, 1).wait_send()
        in_sib(g, 0).wait_send()
        in_sib(g, 1).wait_send()
        back_sib(g).wait_send()
        back_x(g).wait_send()
        for hop, there_in, there_out in ((0, up4, down8), (1, middle, down4)):

            @pl.when(there_in)
            def _(g=g, hop=hop):
                in_z(g, hop).wait_send()

            @pl.when(there_out)
            def _(g=g, hop=hop):
                back_z(g, hop).wait_send()


def on_device(queries, keys, values, out_grad, attn_out, doc_ids):
    ranks = lax.axis_size("ctx")
    rows = queries.shape[0]
    bf16, f32 = jnp.bfloat16, jnp.float32
    vmem = pl.BlockSpec(memory_space=pltpu.VMEM)
    block = (rows, HEAD_DIM)
    pair = (2 * rows, HEAD_DIM)
    return pl.pallas_call(
        functools.partial(kernel, ranks),
        out_shape=(
            jax.ShapeDtypeStruct(queries.shape, bf16),
            jax.ShapeDtypeStruct(keys.shape, bf16),
            jax.ShapeDtypeStruct(values.shape, bf16),
        ),
        in_specs=[pl.BlockSpec(memory_space=pltpu.HBM)] * 6,
        out_specs=(vmem,) * 3,
        scratch_shapes=[
            pltpu.VMEM((KV_HEADS, BLOCKS, 2 * rows + DOC_ROWS, HEAD_DIM), bf16),
            pltpu.VMEM(queries.shape, bf16),
            pltpu.VMEM(queries.shape, bf16),
            pltpu.VMEM(queries.shape, bf16),
            pltpu.VMEM((1, rows), jnp.int32),
            pltpu.VMEM((BLOCKS * rows, 2 * rows), f32),
            pltpu.VMEM((BLOCKS * rows, 2 * rows), bf16),
            pltpu.VMEM((BLOCKS * rows, 2 * rows), bf16),
            pltpu.VMEM((BLOCKS * rows, rows), f32),
            pltpu.VMEM((BLOCKS,) + block, f32),
            pltpu.VMEM((BLOCKS,) + block, f32),
            pltpu.VMEM((2, EVENS) + block, f32),
            pltpu.VMEM((2, EVENS) + block, f32),
            pltpu.VMEM((KV_HEADS, 4) + pair, bf16),
            pltpu.VMEM((KV_HEADS, 4) + pair, bf16),
            pltpu.VMEM((KV_HEADS, 2) + pair, bf16),
            pltpu.VMEM((KV_HEADS, 2) + pair, bf16),
            pltpu.VMEM((KV_HEADS, 2) + pair, bf16),
            pltpu.VMEM((KV_HEADS, 2) + pair, bf16),
            pltpu.SemaphoreType.DMA((KV_HEADS, 6)),
            pltpu.SemaphoreType.DMA((KV_HEADS, 6)),
            pltpu.SemaphoreType.DMA((KV_HEADS, 4)),
            pltpu.SemaphoreType.DMA((KV_HEADS, 4)),
            pltpu.SemaphoreType.DMA((KV_HEADS, 2)),
            pltpu.SemaphoreType.DMA((4,)),
        ],
        compiler_params=pltpu.CompilerParams(
            collective_id=0, has_side_effects=True, vmem_limit_bytes=60 * 1024 * 1024
        ),
    )(queries, keys, values, out_grad, attn_out, doc_ids.reshape(1, rows))


def solution(mesh):
    spec = P(("groups", "ctx"), None)
    return jax.shard_map(
        on_device,
        mesh=mesh,
        in_specs=(spec,) * 5 + (P(("groups", "ctx")),),
        out_specs=(spec,) * 3,
        check_vma=False,
    )
```
